32 devices in a mesh: row: 4 (over y, core), col: 4 (over z), tm: 2 (over x).
Axes of the slice: x: 2, y: 2, z: 4, core: 2. Of those that a mesh axis runs over, the one named last changes fastest.
Arguments:
- counts: float32 [1024, 256, 512], P('row', 'col', 'tm'), may hold values from 0 to 60, as said below
- factor_a: float32 [1024, 32], P('row'), may hold values from 0.05 to 1
- factor_b: float32 [256, 32], P(('col', 'tm')), may hold values from 0.05 to 3, as said below
- factor_c: float32 [512, 32], P('tm'), may hold values from 0.1 to 1
Outputs:
- updated_a: float32 [1024, 32], P(('row', 'col', 'tm'))
The draws below stay inside these ranges and needn't reach their ends.
Inputs may be any that keep to these rules, and one draw needn't show every extreme that they name: `counts`: whole numbers. `factor_b`: positive.
All inputs are finite; a program needn't handle non-finite values.
Results may differ from the reference program's by a relative error of at most 0.00027.
Values sent between devices are 32-bit elements; how exact they have to be, the bound alone decides.
A program may use at most 128 MiB of HBM per device.

```python
import math
import jax
import jax.numpy as jnp
from jax import lax

R = 32
ITERS = 6
I = 1024
J = 256
K = 512


def sparse_levels(key_live, key_level, length, highest, chance):
    active = jax.random.randint(key_live, (length, R), 0, chance) == 0
    levels = jax.random.randint(key_level, (length, R), 1, highest + 1)
    return jnp.where(active, levels, 0).astype(jnp.int32)


def draw_counts(key, part):
    subkeys = jax.random.split(key, 7)
    rows_star = sparse_levels(subkeys[0], subkeys[1], I, 4, 4)
    cols_star = sparse_levels(subkeys[2], subkeys[3], J, 4, 4)
    bins_star = sparse_levels(subkeys[4], subkeys[5], K, 8, 8)
    paired = (rows_star[:, None, :] * cols_star[None, :, :]).reshape(I * J, R)
    planted = jnp.dot(paired, bins_star.T, preferred_element_type=jnp.int32).reshape(I, J, K)
    jitter = jax.random.randint(subkeys[6], (I, J, K), 0, 3)
    return jnp.minimum(planted + jitter, 60).astype(jnp.float32)


def draw_factor_b(key, part):
    rise = 1.0 + 2.0 * jnp.arange(J, dtype=jnp.float32)[:, None] / max(J - 1, 1)
    base = jnp.exp(jax.random.uniform(key, (J, R), jnp.float32, jnp.log(0.1), 0.0))
    return (base * rise).astype(jnp.float32)


def level_of(key, shape, cuts, least, largest):
    def one(axis_at, blocks):
        heights = jax.random.uniform(jax.random.fold_in(jax.random.fold_in(key, 6), axis_at), (blocks,), jnp.float32, least / len(cuts), largest / len(cuts))
        return jnp.repeat(jnp.exp(heights), shape[axis_at] // blocks).reshape((-1,) + (1,) * (len(shape) - axis_at - 1))

    factor_of = one(*cuts[0])
    for cut in cuts[1:]:
        factor_of = factor_of * one(*cut)
    return factor_of


def setup_inputs(seed: int = 0) -> dict:
    splits = jax.random.split(jax.random.key(seed), 5)
    counts = draw_counts(jax.random.fold_in(splits[4], 71), 0)
    factor_a = jnp.clip(jnp.exp(math.log(1.0) - 2.9957323 * jax.random.uniform(splits[1], (I, R), jnp.float32) ** level_of(splits[1], (I, R), ((0, 4),), -0.2, 0.2)), 0.05, 1.0)
    factor_b = draw_factor_b(jax.random.fold_in(splits[4], 71), 0)
    factor_c = jnp.clip(jnp.exp(math.log(1.0) - 2.3025851 * jax.random.uniform(splits[3], (K, R), jnp.float32) ** level_of(splits[3], (K, R), ((0, 2),), -0.2, 0.2)), 0.1, 1.0)
    return {"counts": counts, "factor_a": factor_a, "factor_b": factor_b, "factor_c": factor_c}


def reference(counts, factor_a, factor_b, factor_c):
    sum_b = jnp.sum(factor_b, axis=0)
    sum_c = jnp.sum(factor_c, axis=0)
    norm_b = factor_b / (sum_b / J)
    norm_c = factor_c / (sum_c / K)
    kr = (norm_b.T[:, :, None] * norm_c.T[:, None, :]).reshape(R, J * K)
    flat = counts.reshape(I, J * K)
    block = math.gcd(I, 64)

    def one_block(pair):
        rows, weights = pair
        model = jnp.dot(weights, kr, precision=lax.Precision.HIGHEST, preferred_element_type=jnp.float32)
        ratio = rows / model
        total = lax.dot_general(ratio, kr, (((1,), (1,)), ((), ())), precision=lax.Precision.HIGHEST, preferred_element_type=jnp.float32)
        return total / float(J * K)

    current = factor_a
    for step in range(ITERS):
        phi = lax.map(one_block, (flat.reshape(I // block, block, J * K), current.reshape(I // block, block, R)))
        current = current * phi.reshape(I, R)
    return current
```

```python
import functools

import jax
import jax.numpy as jnp
from jax import lax
from jax.experimental import pallas as pl
from jax.experimental.pallas import tpu as pltpu
from jax.sharding import PartitionSpec as P

ITERS = 6
MESH = pl.DeviceIdType.MESH
BF16 = jnp.bfloat16
F32 = jnp.float32


def kernel(
    cols, tms, blocks, rows,
    counts_hbm, a_ref, b_ref, c_ref, out_ref,
    counts_v, cur, part, recv, sums, b_all, norm_b, c_in, c_out,
    counts_sem, sums_send, sums_recv, b_send, b_recv,
    rs_send, rs_recv, ag_send, ag_recv,
):
    group = cols * tms
    my_col, my_tm = lax.axis_index("col"), lax.axis_index("tm")
    me = my_col * tms + my_tm
    rank = a_ref.shape[1]
    copies = 128 // rank
    j_own = b_ref.shape[0]
    j_local = j_own * tms
    k_local = c_ref.shape[0]
    whole_j = j_local * cols
    whole_k = k_local * tms
    cells = float(whole_j * whole_k)

    def peer(d):
        return lax.rem(me + d, group)

    def device(p):
        return {"col": lax.div(p, tms), "tm": lax.rem(p, tms)}

    def load(b):
        return pltpu.make_async_copy(
            counts_hbm.at[:, b], counts_v.at[:, b], counts_sem.at[b]
        )

    for b in range(blocks):
        load(b).start()

    barrier = pltpu.get_barrier_semaphore()
    for d in range(1, group):
        pl.semaphore_signal(barrier, inc=1, device_id=device(peer(d)), device_id_type=MESH)

    b_wide = jnp.concatenate([b_ref[...]] * copies, axis=1)
    c_wide = jnp.concatenate([c_ref[...]] * copies, axis=1)
    b_sum = jnp.sum(b_wide, axis=0, keepdims=True)
    c_sum = jnp.sum(c_wide, axis=0, keepdims=True)
    line = lax.broadcasted_iota(jnp.int32, (8, 128), 0)
    b_all[my_tm] = b_wide
    sums[me] = jnp.where(line == 0, b_sum, c_sum)
    a_wide = jnp.concatenate([a_ref[...]] * copies, axis=1)
    cur[...] = a_wide.reshape(cur.shape)

    pl.semaphore_wait(barrier, group - 1)

    def send_sums(p, q):
        return pltpu.make_async_remote_copy(
            src_ref=sums.at[q], dst_ref=sums.at[q],
            send_sem=sums_send.at[p], recv_sem=sums_recv.at[q],
            device_id=device(p), device_id_type=MESH,
        )

    def send_b(t, owner):
        return pltpu.make_async_remote_copy(
            src_ref=b_all.at[owner], dst_ref=b_all.at[owner],
            send_sem=b_send.at[t], recv_sem=b_recv.at[owner],
            device_id={"tm": t}, device_id_type=MESH,
        )

    for d in range(1, group):
        send_sums(peer(d), me).start()
    for d in range(1, tms):
        send_b(lax.rem(my_tm + d, tms), my_tm).start()
    for d in range(1, group):
        send_sums(peer(d), peer(d)).wait_recv()
    for d in range(1, tms):
        other = lax.rem(my_tm + d, tms)
        send_b(other, other).wait_recv()

    all_sums = jnp.sum(sums[...], axis=0)
    sum_b = all_sums[0:1]
    sum_c = all_sums[1:2] / cols
    norm_b[...] = b_all[...].reshape(j_local, 128) / (sum_b / whole_j)
    c_norm = c_wide / (sum_c / whole_k)
    c_high = c_norm.astype(BF16).astype(F32)
    c_low = c_norm - c_high
    lane = lax.broadcasted_iota(jnp.int32, (k_local, 128), 1) // rank
    mixed = jnp.where(lane % 2 == 0, c_high, c_low)
    c_in[...] = mixed.T.astype(BF16)
    once = jnp.where(lane < 2, mixed, 0.0).astype(BF16)
    c_out[0:k_local] = once
    c_out[k_local : 2 * k_local] = once

    for d in range(1, group):
        send_sums(peer(d), me).wait_send()
    for d in range(1, tms):
        send_b(lax.rem(my_tm + d, tms), my_tm).wait_send()

    def send_part(p, q, b):
        return pltpu.make_async_remote_copy(
            src_ref=part.at[p, b], dst_ref=recv.at[q, b],
            send_sem=rs_send.at[p, b], recv_sem=rs_recv.at[q, b],
            device_id=device(p), device_id_type=MESH,
        )

    def send_cur(p, q, b):
        return pltpu.make_async_remote_copy(
            src_ref=cur.at[q, b], dst_ref=cur.at[q, b],
            send_sem=ag_send.at[p, b], recv_sem=ag_recv.at[q, b],
            device_id=device(p), device_id_type=MESH,
        )

    def chunk(p, b):
        weights = norm_b[...]
        first = cur[p, b][:, None, :] * weights[None]
        first = first.reshape(rows * j_local, 128)
        high = first.astype(BF16).astype(F32)
        lanes = lax.broadcasted_iota(jnp.int32, first.shape, 1)
        left = jnp.where(lanes < 2 * rank, first, first - high).astype(BF16)
        model = jnp.dot(left, c_in[...], preferred_element_type=F32)
        x = counts_v[p, b].reshape(rows * j_local, k_local)
        inverse = pl.reciprocal(model, approx=True)
        ratio_high = (x * inverse).astype(BF16)
        ratio_low = ((x - model * ratio_high.astype(F32)) * inverse).astype(BF16)
        ratio = jnp.concatenate([ratio_high, ratio_low], axis=1)
        inner = jnp.dot(ratio, c_out[...], preferred_element_type=F32)
        inner = inner.reshape(rows, j_local, 128) * weights[None]
        part[p, b] = jnp.sum(inner, axis=1)

    def finish(u):
        b = lax.rem(u, blocks)
        for d in range(1, group):
            send_part(peer(d), peer(d), b).wait_recv()

        @pl.when(u >= blocks)
        def _():
            for d in range(1, group):
                send_cur(peer(d), me, b).wait_send()

        total = part[me, b]
        for d in range(1, group):
            total = total + recv[peer(d), b]
        width = 64
        while width >= rank:
            total = total + pltpu.roll(total, width, 1)
            width //= 2
        new = cur[me, b] * (total / cells)
        cur[me, b] = new

        @pl.when(u < (ITERS - 1) * blocks)
        def _():
            for d in range(1, group):
                send_cur(peer(d), me, b).start()

    lag = 1 if blocks > 1 else 0
    steps = ITERS * blocks

    def step(s, carry):
        b = lax.rem(s, blocks)

        @pl.when(s < blocks)
        def _():
            load(b).wait()

        @pl.when(s >= blocks)
        def _():
            for d in range(1, group):
                send_cur(peer(d), peer(d), b).wait_recv()
                send_part(peer(d), me, b).wait_send()

        def one(d, carry):
            p = peer(d)
            chunk(p, b)

            @pl.when(d < group)
            def _():
                send_part(p, me, b).start()

            return carry

        lax.fori_loop(1, group + 1, one, 0)

        @pl.when(s >= lag)
        def _():
            finish(s - lag)

        return carry

    lax.fori_loop(0, steps, step, 0)
    if lag:
        finish(steps - 1)
    for b in range(blocks):
        for d in range(1, group):
            send_part(peer(d), me, b).wait_send()
        out_ref[b * rows : (b + 1) * rows, :] = cur[me, b][:, 0:rank]


def per_device(counts, factor_a, factor_b, factor_c):
    cols, tms = lax.axis_size("col"), lax.axis_size("tm")
    group = cols * tms
    rows_local, j_local, k_local = counts.shape
    rank = factor_a.shape[1]
    own = rows_local // group
    rows = 8 if own % 8 == 0 else own
    blocks = own // rows
    counts = counts.reshape(group, blocks, rows, j_local, k_local)
    cells = rows_local * j_local * k_local
    vmem = pl.BlockSpec(memory_space=pltpu.VMEM)
    dma = pltpu.SemaphoreType.DMA
    return pl.pallas_call(
        functools.partial(kernel, cols, tms, blocks, rows),
        out_shape=jax.ShapeDtypeStruct((own, rank), F32),
        in_specs=[pl.BlockSpec(memory_space=pl.ANY), vmem, vmem, vmem],
        out_specs=vmem,
        scratch_shapes=[
            pltpu.VMEM(counts.shape, F32),
            pltpu.VMEM((group, blocks, rows, 128), F32),
            pltpu.VMEM((group, blocks, rows, 128), F32),
            pltpu.VMEM((group, blocks, rows, 128), F32),
            pltpu.VMEM((group, 8, 128), F32),
            pltpu.VMEM((tms, j_local // tms, 128), F32),
            pltpu.VMEM((j_local, 128), F32),
            pltpu.VMEM((128, k_local), BF16),
            pltpu.VMEM((2 * k_local, 128), BF16),
            dma((blocks,)),
            dma((group,)),
            dma((group,)),
            dma((tms,)),
            dma((tms,)),
            dma((group, blocks)),
            dma((group, blocks)),
            dma((group, blocks)),
            dma((group, blocks)),
        ],
        compiler_params=pltpu.CompilerParams(
            collective_id=0, has_side_effects=True, vmem_limit_bytes=48 * 1024 * 1024
        ),
        cost_estimate=pl.CostEstimate(
            flops=4 * ITERS * cells * rank,
            bytes_accessed=4 * cells,
            transcendentals=ITERS * cells,
        ),
    )(counts, factor_a, factor_b, factor_c)


def solution(mesh):
    return jax.shard_map(
        per_device,
        mesh=mesh,
        in_specs=(P("row", "col", "tm"), P("row", None), P(("col", "tm"), None), P("tm", None)),
        out_specs=P(("row", "col", "tm"), None),
        check_vma=False,
    )
```

```python
import functools

import jax
import jax.numpy as jnp
from jax import lax
from jax.experimental import pallas as pl
from jax.experimental.pallas import tpu as pltpu
from jax.sharding import PartitionSpec as P

ITERS = 6
MESH = pl.DeviceIdType.MESH
BF16 = jnp.bfloat16
F32 = jnp.float32


def kernel(
    cols, tms, blocks, rows, pieces,
    counts_hbm, a_ref, b_ref, c_ref, out_ref,
    counts_v, cur, part, recv, sums, b_all, norm_b, c_in, c_out,
    counts_sem, sums_send, sums_recv, b_send, b_recv,
    rs_send, rs_recv, ag_send, ag_recv,
):
    group = cols * tms
    my_col, my_tm = lax.axis_index("col"), lax.axis_index("tm")
    me = my_col * tms + my_tm
    rank = a_ref.shape[1]
    copies = 128 // rank
    j_own = b_ref.shape[0]
    j_local = j_own * tms
    k_local = c_ref.shape[0]
    whole_j = j_local * cols
    whole_k = k_local * tms
    cells = float(whole_j * whole_k)

    def peer(d):
        return lax.rem(me + d, group)

    def device(p):
        return {"col": lax.div(p, tms), "tm": lax.rem(p, tms)}

    def load(b):
        return pltpu.make_async_copy(
            counts_hbm.at[:, b], counts_v.at[:, b], counts_sem.at[b]
        )

    for b in range(blocks):
        load(b).start()

    barrier = pltpu.get_barrier_semaphore()
    for d in range(1, group):
        pl.semaphore_signal(barrier, inc=1, device_id=device(peer(d)), device_id_type=MESH)

    b_wide = jnp.concatenate([b_ref[...]] * copies, axis=1)
    c_wide = jnp.concatenate([c_ref[...]] * copies, axis=1)
    b_sum = jnp.sum(b_wide, axis=0, keepdims=True)
    c_sum = jnp.sum(c_wide, axis=0, keepdims=True)
    line = lax.broadcasted_iota(jnp.int32, (8, 128), 0)
    b_all[my_tm] = b_wide
    sums[me] = jnp.where(line == 0, b_sum, c_sum)
    a_wide = jnp.concatenate([a_ref[...]] * copies, axis=1)
    for p in range(group):
        for b in range(blocks):
            start = (p * blocks + b) * rows
            cur[b, p] = a_wide[start : start + rows]

    pl.semaphore_wait(barrier, group - 1)

    def send_sums(p, q):
        return pltpu.make_async_remote_copy(
            src_ref=sums.at[q], dst_ref=sums.at[q],
            send_sem=sums_send.at[p], recv_sem=sums_recv.at[q],
            device_id=device(p), device_id_type=MESH,
        )

    def send_b(t, owner):
        return pltpu.make_async_remote_copy(
            src_ref=b_all.at[owner], dst_ref=b_all.at[owner],
            send_sem=b_send.at[t], recv_sem=b_recv.at[owner],
            device_id={"tm": t}, device_id_type=MESH,
        )

    for d in range(1, group):
        send_sums(peer(d), me).start()
    for d in range(1, tms):
        send_b(lax.rem(my_tm + d, tms), my_tm).start()
    for d in range(1, group):
        send_sums(peer(d), peer(d)).wait_recv()
    for d in range(1, tms):
        other = lax.rem(my_tm + d, tms)
        send_b(other, other).wait_recv()

    all_sums = jnp.sum(sums[...], axis=0)
    sum_b = all_sums[0:1]
    sum_c = all_sums[1:2] / cols
    norm_b[...] = b_all[...].reshape(j_local, 128) / (sum_b / whole_j)
    c_norm = c_wide / (sum_c / whole_k)
    c_high = c_norm.astype(BF16).astype(F32)
    c_low = c_norm - c_high
    lane = lax.broadcasted_iota(jnp.int32, (k_local, 128), 1) // rank
    mixed = jnp.where(lane % 2 == 0, c_high, c_low)
    c_in[...] = mixed.T.astype(BF16)
    once = jnp.where(lane < 2, mixed, 0.0).astype(BF16)
    c_out[...] = once

    for d in range(1, group):
        send_sums(peer(d), me).wait_send()
    for d in range(1, tms):
        send_b(lax.rem(my_tm + d, tms), my_tm).wait_send()

    def send_part(p, q, b):
        return pltpu.make_async_remote_copy(
            src_ref=part.at[b, p], dst_ref=recv.at[b, q],
            send_sem=rs_send.at[b], recv_sem=rs_recv.at[b],
            device_id=device(p), device_id_type=MESH,
        )

    def send_cur(p, q, b):
        return pltpu.make_async_remote_copy(
            src_ref=cur.at[b, q], dst_ref=cur.at[b, q],
            send_sem=ag_send.at[b], recv_sem=ag_recv.at[b],
            device_id=device(p), device_id_type=MESH,
        )

    def wait_all(ref, sem, b):
        pages = ref.at[b, pl.ds(0, group - 1)]
        pltpu.make_async_copy(pages, pages, sem.at[b]).wait()

    sub = rows // pieces
    sub_rows = sub * j_local

    def expand(p, b, h):
        first = cur[b, p, h * sub : (h + 1) * sub][:, None, :] * norm_b[...][None]
        first = first.reshape(sub_rows, 128)
        high = first.astype(BF16).astype(F32)
        lanes = lax.broadcasted_iota(jnp.int32, first.shape, 1)
        left = jnp.where(lanes < 2 * rank, first, first - high).astype(BF16)
        return jnp.dot(left, c_in[...], preferred_element_type=F32)

    def divide(p, b, h, model):
        x = counts_v[p, b, h * sub : (h + 1) * sub].reshape(sub_rows, k_local)
        inverse = pl.reciprocal(model, approx=True)
        ratio_high = (x * inverse).astype(BF16)
        ratio_low = ((x - model * ratio_high.astype(F32)) * inverse).astype(BF16)
        return ratio_high, ratio_low

    def collect(ratio_high, ratio_low):
        split = []
        for i in range(sub):
            split += [ratio_high[i * j_local : (i + 1) * j_local]]
            split += [ratio_low[i * j_local : (i + 1) * j_local]]
        inner = jnp.dot(
            jnp.concatenate(split, axis=0), c_out[...], preferred_element_type=F32
        ).reshape(sub, 2, j_local, 128)
        return jnp.sum((inner[:, 0] + inner[:, 1]) * norm_b[...][None], axis=1)

    def chunk(p, b):
        models = [expand(p, b, 0)]
        sums_of = []
        for h in range(pieces):
            if h + 1 < pieces:
                models.append(expand(p, b, h + 1))
            sums_of.append(collect(*divide(p, b, h, models[h])))
        part[b, p] = jnp.concatenate(sums_of, axis=0)

    def finish(u):
        b = lax.rem(u, blocks)
        wait_all(recv, rs_recv, b)

        @pl.when(u >= blocks)
        def _():
            wait_all(cur, ag_send, b)

        total = part[b, me]
        for d in range(1, group):
            total = total + recv[b, peer(d)]
        width = 64
        while width >= rank:
            total = total + pltpu.roll(total, width, 1)
            width //= 2
        cur[b, me] = cur[b, me] * (total / cells)

        @pl.when(u < (ITERS - 1) * blocks)
        def _():
            for d in range(1, group):
                send_cur(peer(d), me, b).start()

    steps = ITERS * blocks

    def step(s, carry):
        b = lax.rem(s, blocks)

        @pl.when(s < blocks)
        def _():
            load(b).wait()

        @pl.when(s >= blocks)
        def _():
            wait_all(cur, ag_recv, b)
            wait_all(part, rs_send, b)

        def one(d, carry):
            p = peer(d)
            chunk(p, b)

            @pl.when(d < group)
            def _():
                send_part(p, me, b).start()

            return carry

        lax.fori_loop(1, group // 2 + 1, one, 0)
        if blocks > 1:

            @pl.when(s >= 1)
            def _():
                finish(s - 1)

        lax.fori_loop(group // 2 + 1, group + 1, one, 0)
        if blocks == 1:
            finish(s)
        return carry

    lax.fori_loop(0, steps, step, 0)
    if blocks > 1:
        finish(steps - 1)
    for b in range(blocks):
        wait_all(part, rs_send, b)
        out_ref[b * rows : (b + 1) * rows, :] = cur[b, me][:, 0:rank]


def per_device(counts, factor_a, factor_b, factor_c):
    cols, tms = lax.axis_size("col"), lax.axis_size("tm")
    group = cols * tms
    rows_local, j_local, k_local = counts.shape
    rank = factor_a.shape[1]
    own = rows_local // group
    blocks = 2 if own % 16 == 0 else 1
    rows = own // blocks
    pieces = max(1, rows // 4)
    counts = counts.reshape(group, blocks, rows, j_local, k_local)
    cells = rows_local * j_local * k_local
    vmem = pl.BlockSpec(memory_space=pltpu.VMEM)
    dma = pltpu.SemaphoreType.DMA
    return pl.pallas_call(
        functools.partial(kernel, cols, tms, blocks, rows, pieces),
        out_shape=jax.ShapeDtypeStruct((own, rank), F32),
        in_specs=[pl.BlockSpec(memory_space=pl.ANY), vmem, vmem, vmem],
        out_specs=vmem,
        scratch_shapes=[
            pltpu.VMEM(counts.shape, F32),
            pltpu.VMEM((blocks, group, rows, 128), F32),
            pltpu.VMEM((blocks, group, rows, 128), F32),
            pltpu.VMEM((blocks, group, rows, 128), F32),
            pltpu.VMEM((group, 8, 128), F32),
            pltpu.VMEM((tms, j_local // tms, 128), F32),
            pltpu.VMEM((j_local, 128), F32),
            pltpu.VMEM((128, k_local), BF16),
            pltpu.VMEM((k_local, 128), BF16),
            dma((blocks,)),
            dma((group,)),
            dma((group,)),
            dma((tms,)),
            dma((tms,)),
            dma((blocks,)),
            dma((blocks,)),
            dma((blocks,)),
            dma((blocks,)),
        ],
        compiler_params=pltpu.CompilerParams(
            collective_id=0, has_side_effects=True, vmem_limit_bytes=48 * 1024 * 1024
        ),
        cost_estimate=pl.CostEstimate(
            flops=4 * ITERS * cells * rank,
            bytes_accessed=4 * cells,
            transcendentals=ITERS * cells,
        ),
    )(counts, factor_a, factor_b, factor_c)


def solution(mesh):
    return jax.shard_map(
        per_device,
        mesh=mesh,
        in_specs=(P("row", "col", "tm"), P("row", None), P(("col", "tm"), None), P("tm", None)),
        out_specs=P(("row", "col", "tm"), None),
        check_vma=False,
    )
```

```python
import functools

import jax
import jax.numpy as jnp
from jax import lax
from jax.experimental import pallas as pl
from jax.experimental.pallas import tpu as pltpu
from jax.sharding import PartitionSpec as P

ITERS = 6
MESH = pl.DeviceIdType.MESH
BF16 = jnp.bfloat16
F32 = jnp.float32


def kernel(
    cols, tms, blocks, rows, pieces,
    counts_hbm, a_hbm, b_hbm, c_hbm, out_ref,
    a_ref, b_ref, c_ref,
    counts_v, cur, part, recv, sums, b_all, norm_b, c_in, c_out,
    factor_sem, counts_sem, sums_send, sums_recv, b_send, b_recv,
    rs_send, rs_recv, ag_send, ag_recv,
):
    group = cols * tms
    my_col, my_tm = lax.axis_index("col"), lax.axis_index("tm")
    me = my_col * tms + my_tm
    rank = a_ref.shape[0]
    copies = 128 // rank
    j_own = b_ref.shape[0]
    j_local = j_own * tms
    k_local = c_ref.shape[1]
    whole_j = j_local * cols
    whole_k = k_local * tms
    cells = float(whole_j * whole_k)

    def peer(d):
        return lax.rem(me + d, group)

    def device(p):
        return {"col": lax.div(p, tms), "tm": lax.rem(p, tms)}

    def load(b):
        return pltpu.make_async_copy(
            counts_hbm.at[:, b], counts_v.at[:, b], counts_sem.at[b]
        )

    factors = [
        pltpu.make_async_copy(source, target, factor_sem.at[i])
        for i, (source, target) in enumerate(
            [(b_hbm, b_ref), (c_hbm, c_ref), (a_hbm, a_ref)]
        )
    ]
    for copy in factors:
        copy.start()
    for b in range(blocks):
        load(b).start()

    barrier = pltpu.get_barrier_semaphore()
    for d in range(1, group):
        pl.semaphore_signal(barrier, inc=1, device_id=device(peer(d)), device_id_type=MESH)

    for copy in factors:
        copy.wait()
    b_wide = jnp.concatenate([b_ref[...]] * copies, axis=1)
    c_wide = jnp.concatenate([c_ref[...]] * copies, axis=0).T
    b_sum = jnp.sum(b_wide, axis=0, keepdims=True)
    c_sum = jnp.sum(c_wide, axis=0, keepdims=True)
    line = lax.broadcasted_iota(jnp.int32, (8, 128), 0)
    b_all[my_tm] = b_wide
    sums[me] = jnp.where(line == 0, b_sum, c_sum)
    a_wide = jnp.concatenate([a_ref[...]] * copies, axis=0).T
    for p in range(group):
        for b in range(blocks):
            start = (p * blocks + b) * rows
            cur[b, p] = a_wide[start : start + rows]

    pl.semaphore_wait(barrier, group - 1)

    def send_sums(p, q):
        return pltpu.make_async_remote_copy(
            src_ref=sums.at[q], dst_ref=sums.at[q],
            send_sem=sums_send.at[p], recv_sem=sums_recv.at[q],
            device_id=device(p), device_id_type=MESH,
        )

    def send_b(t, owner):
        return pltpu.make_async_remote_copy(
            src_ref=b_all.at[owner], dst_ref=b_all.at[owner],
            send_sem=b_send.at[t], recv_sem=b_recv.at[owner],
            device_id={"tm": t}, device_id_type=MESH,
        )

    for d in range(1, group):
        send_sums(peer(d), me).start()
    for d in range(1, tms):
        send_b(lax.rem(my_tm + d, tms), my_tm).start()
    for d in range(1, group):
        send_sums(peer(d), peer(d)).wait_recv()
    for d in range(1, tms):
        other = lax.rem(my_tm + d, tms)
        send_b(other, other).wait_recv()

    all_sums = jnp.sum(sums[...], axis=0)
    sum_b = all_sums[0:1]
    sum_c = all_sums[1:2] / cols
    norm_b[...] = b_all[...].reshape(j_local, 128) / (sum_b / whole_j)
    c_norm = c_wide / (sum_c / whole_k)
    c_high = c_norm.astype(BF16).astype(F32)
    c_low = c_norm - c_high
    lane = lax.broadcasted_iota(jnp.int32, (k_local, 128), 1) // rank
    mixed = jnp.where(lane % 2 == 0, c_high, c_low)
    c_in[...] = mixed.T.astype(BF16)
    once = jnp.where(lane < 2, mixed, 0.0).astype(BF16)
    c_out[...] = once

    for d in range(1, group):
        send_sums(peer(d), me).wait_send()
    for d in range(1, tms):
        send_b(lax.rem(my_tm + d, tms), my_tm).wait_send()

    def send_part(p, q, b):
        return pltpu.make_async_remote_copy(
            src_ref=part.at[b, p], dst_ref=recv.at[b, q],
            send_sem=rs_send.at[b], recv_sem=rs_recv.at[b],
            device_id=device(p), device_id_type=MESH,
        )

    def send_cur(p, q, b):
        return pltpu.make_async_remote_copy(
            src_ref=cur.at[b, q], dst_ref=cur.at[b, q],
            send_sem=ag_send.at[b], recv_sem=ag_recv.at[b],
            device_id=device(p), device_id_type=MESH,
        )

    def wait_all(ref, sem, b):
        pages = ref.at[b, pl.ds(0, group - 1)]
        pltpu.make_async_copy(pages, pages, sem.at[b]).wait()

    sub = rows // pieces
    sub_rows = sub * j_local

    def expand(p, b, h):
        first = cur[b, p, h * sub : (h + 1) * sub][:, None, :] * norm_b[...][None]
        first = first.reshape(sub_rows, 128)
        high = first.astype(BF16).astype(F32)
        lanes = lax.broadcasted_iota(jnp.int32, first.shape, 1)
        left = jnp.where(lanes < 2 * rank, first, first - high).astype(BF16)
        return jnp.dot(left, c_in[...], preferred_element_type=F32)

    def divide(p, b, h, model):
        x = counts_v[p, b, h * sub : (h + 1) * sub].reshape(sub_rows, k_local)
        inverse = pl.reciprocal(model, approx=True)
        ratio_high = (x * inverse).astype(BF16)
        ratio_low = ((x - model * ratio_high.astype(F32)) * inverse).astype(BF16)
        return ratio_high, ratio_low

    def collect(ratio_high, ratio_low):
        split = []
        for i in range(sub):
            split += [ratio_high[i * j_local : (i + 1) * j_local]]
            split += [ratio_low[i * j_local : (i + 1) * j_local]]
        inner = jnp.dot(
            jnp.concatenate(split, axis=0), c_out[...], preferred_element_type=F32
        ).reshape(sub, 2, j_local, 128)
        return jnp.sum((inner[:, 0] + inner[:, 1]) * norm_b[...][None], axis=1)

    def chunk(p, b):
        models = [expand(p, b, 0)]
        sums_of = []
        for h in range(pieces):
            if h + 1 < pieces:
                models.append(expand(p, b, h + 1))
            sums_of.append(collect(*divide(p, b, h, models[h])))
        part[b, p] = jnp.concatenate(sums_of, axis=0)

    def finish(u):
        b = lax.rem(u, blocks)
        wait_all(recv, rs_recv, b)

        @pl.when(u >= blocks)
        def _():
            wait_all(cur, ag_send, b)

        total = part[b, me]
        for d in range(1, group):
            total = total + recv[b, peer(d)]
        width = 64
        while width >= rank:
            total = total + pltpu.roll(total, width, 1)
            width //= 2
        cur[b, me] = cur[b, me] * (total / cells)

        @pl.when(u < (ITERS - 1) * blocks)
        def _():
            for d in range(1, group):
                send_cur(peer(d), me, b).start()

    steps = ITERS * blocks

    def step(s, carry):
        b = lax.rem(s, blocks)

        @pl.when(s < blocks)
        def _():
            load(b).wait()

        @pl.when(s >= blocks)
        def _():
            wait_all(cur, ag_recv, b)
            wait_all(part, rs_send, b)

        def one(d, carry):
            p = peer(d)
            chunk(p, b)

            @pl.when(d < group)
            def _():
                send_part(p, me, b).start()

            return carry

        lax.fori_loop(1, group // 2 + 1, one, 0)
        if blocks > 1:

            @pl.when(s >= 1)
            def _():
                finish(s - 1)

        lax.fori_loop(group // 2 + 1, group + 1, one, 0)
        if blocks == 1:
            finish(s)
        return carry

    lax.fori_loop(0, steps, step, 0)
    if blocks > 1:
        finish(steps - 1)
    for b in range(blocks):
        wait_all(part, rs_send, b)
        out_ref[b * rows : (b + 1) * rows, :] = cur[b, me][:, 0:rank]


def per_device(counts, factor_a, factor_b, factor_c):
    cols, tms = lax.axis_size("col"), lax.axis_size("tm")
    group = cols * tms
    rows_local, j_local, k_local = counts.shape
    rank = factor_a.shape[1]
    own = rows_local // group
    blocks = 2 if own % 16 == 0 else 1
    rows = own // blocks
    pieces = max(1, rows // 8)
    counts = counts.reshape(group, blocks, rows, j_local, k_local)
    cells = rows_local * j_local * k_local
    vmem = pl.BlockSpec(memory_space=pltpu.VMEM)
    dma = pltpu.SemaphoreType.DMA
    return pl.pallas_call(
        functools.partial(kernel, cols, tms, blocks, rows, pieces),
        out_shape=jax.ShapeDtypeStruct((own, rank), F32),
        in_specs=[pl.BlockSpec(memory_space=pltpu.HBM)] * 4,
        out_specs=vmem,
        scratch_shapes=[
            pltpu.VMEM((rank, rows_local), F32),
            pltpu.VMEM(factor_b.shape, F32),
            pltpu.VMEM((rank, k_local), F32),
            pltpu.VMEM(counts.shape, F32),
            pltpu.VMEM((blocks, group, rows, 128), F32),
            pltpu.VMEM((blocks, group, rows, 128), F32),
            pltpu.VMEM((blocks, group, rows, 128), F32),
            pltpu.VMEM((group, 8, 128), F32),
            pltpu.VMEM((tms, j_local // tms, 128), F32),
            pltpu.VMEM((j_local, 128), F32),
            pltpu.VMEM((128, k_local), BF16),
            pltpu.VMEM((k_local, 128), BF16),
            dma((3,)),
            dma((blocks,)),
            dma((group,)),
            dma((group,)),
            dma((tms,)),
            dma((tms,)),
            dma((blocks,)),
            dma((blocks,)),
            dma((blocks,)),
            dma((blocks,)),
        ],
        compiler_params=pltpu.CompilerParams(
            collective_id=0, has_side_effects=True, vmem_limit_bytes=48 * 1024 * 1024
        ),
        cost_estimate=pl.CostEstimate(
            flops=4 * ITERS * cells * rank,
            bytes_accessed=4 * cells,
            transcendentals=ITERS * cells,
        ),
    )(counts, factor_a.T, factor_b, factor_c.T)


def solution(mesh):
    return jax.shard_map(
        per_device,
        mesh=mesh,
        in_specs=(P("row", "col", "tm"), P("row", None), P(("col", "tm"), None), P("tm", None)),
        out_specs=P(("row", "col", "tm"), None),
        check_vma=False,
    )
```

```python
import functools

import jax
import jax.numpy as jnp
from jax import lax
from jax.experimental import pallas as pl
from jax.experimental.pallas import tpu as pltpu
from jax.sharding import PartitionSpec as P

ITERS = 6
MESH = pl.DeviceIdType.MESH
BF16 = jnp.bfloat16
F32 = jnp.float32


def kernel(
    cols, tms, blocks, rows, pieces,
    counts_hbm, a_hbm, b_hbm, c_hbm, out_ref,
    a_ref, b_ref, c_ref,
    counts_v, cur, part, recv, sums, b_all, norm_b, c_in, c_out,
    factor_sem, counts_sem, sums_send, sums_recv, b_send, b_recv,
    rs_send, rs_recv, ag_send, ag_recv,
):
    group = cols * tms
    my_col, my_tm = lax.axis_index("col"), lax.axis_index("tm")
    me = my_col * tms + my_tm
    rank = a_ref.shape[0]
    copies = 128 // rank
    j_own = b_ref.shape[0]
    j_local = j_own * tms
    k_local = c_ref.shape[1]
    whole_j = j_local * cols
    whole_k = k_local * tms
    cells = float(whole_j * whole_k)

    def peer(d):
        return lax.rem(me + d, group)

    def device(p):
        return {"col": lax.div(p, tms), "tm": lax.rem(p, tms)}

    def load(b):
        return pltpu.make_async_copy(
            counts_hbm.at[:, b], counts_v.at[:, b], counts_sem.at[b]
        )

    factors = [
        pltpu.make_async_copy(source, target, factor_sem.at[i])
        for i, (source, target) in enumerate(
            [(b_hbm, b_ref), (c_hbm, c_ref), (a_hbm, a_ref)]
        )
    ]
    for copy in factors:
        copy.start()
    for b in range(blocks):
        load(b).start()

    barrier = pltpu.get_barrier_semaphore()
    for d in range(1, group):
        pl.semaphore_signal(barrier, inc=1, device_id=device(peer(d)), device_id_type=MESH)

    for copy in factors:
        copy.wait()
    b_wide = jnp.concatenate([b_ref[...]] * copies, axis=1)
    c_wide = jnp.concatenate([c_ref[...]] * copies, axis=0).T
    b_sum = jnp.sum(b_wide, axis=0, keepdims=True)
    c_sum = jnp.sum(c_wide, axis=0, keepdims=True)
    line = lax.broadcasted_iota(jnp.int32, (8, 128), 0)
    b_all[my_tm] = b_wide
    sums[me] = jnp.where(line == 0, b_sum, c_sum)
    a_wide = jnp.concatenate([a_ref[...]] * copies, axis=0).T
    for p in range(group):
        for b in range(blocks):
            start = (p * blocks + b) * rows
            cur[b, p] = a_wide[start : start + rows]

    pl.semaphore_wait(barrier, group - 1)

    def send_sums(p, q):
        return pltpu.make_async_remote_copy(
            src_ref=sums.at[q], dst_ref=sums.at[q],
            send_sem=sums_send.at[p], recv_sem=sums_recv.at[q],
            device_id=device(p), device_id_type=MESH,
        )

    def send_b(t, owner):
        return pltpu.make_async_remote_copy(
            src_ref=b_all.at[owner], dst_ref=b_all.at[owner],
            send_sem=b_send.at[t], recv_sem=b_recv.at[owner],
            device_id={"tm": t}, device_id_type=MESH,
        )

    for d in range(1, group):
        send_sums(peer(d), me).start()
    for d in range(1, tms):
        send_b(lax.rem(my_tm + d, tms), my_tm).start()
    for d in range(1, group):
        send_sums(peer(d), peer(d)).wait_recv()
    for d in range(1, tms):
        other = lax.rem(my_tm + d, tms)
        send_b(other, other).wait_recv()

    all_sums = jnp.sum(sums[...], axis=0)
    sum_b = all_sums[0:1]
    sum_c = all_sums[1:2] / cols
    norm_b[...] = b_all[...].reshape(j_local, 128) / (sum_b / whole_j)
    c_norm = c_wide / (sum_c / whole_k)
    c_high = c_norm.astype(BF16).astype(F32)
    c_low = c_norm - c_high
    lane = lax.broadcasted_iota(jnp.int32, (k_local, 128), 1) // rank
    mixed = jnp.where(lane % 2 == 0, c_high, c_low)
    c_in[...] = mixed.T.astype(BF16)
    once = jnp.where(lane < 2, mixed, 0.0).astype(BF16)
    c_out[...] = once

    for d in range(1, group):
        send_sums(peer(d), me).wait_send()
    for d in range(1, tms):
        send_b(lax.rem(my_tm + d, tms), my_tm).wait_send()

    def send_part(p, q, b):
        return pltpu.make_async_remote_copy(
            src_ref=part.at[b, p], dst_ref=recv.at[b, q],
            send_sem=rs_send.at[b], recv_sem=rs_recv.at[b],
            device_id=device(p), device_id_type=MESH,
        )

    def send_cur(p, q, b):
        return pltpu.make_async_remote_copy(
            src_ref=cur.at[b, q], dst_ref=cur.at[b, q],
            send_sem=ag_send.at[b], recv_sem=ag_recv.at[b],
            device_id=device(p), device_id_type=MESH,
        )

    def wait_all(ref, sem, b):
        pages = ref.at[b, pl.ds(0, group - 1)]
        pltpu.make_async_copy(pages, pages, sem.at[b]).wait()

    sub = rows // pieces
    sub_rows = sub * j_local

    def expand(p, b, h):
        first = cur[b, p, h * sub : (h + 1) * sub][:, None, :] * norm_b[...][None]
        first = first.reshape(sub_rows, 128)
        high = first.astype(BF16).astype(F32)
        lanes = lax.broadcasted_iota(jnp.int32, first.shape, 1)
        left = jnp.where(lanes < 2 * rank, first, first - high).astype(BF16)
        return jnp.dot(left, c_in[...], preferred_element_type=F32)

    def divide(p, b, h, model):
        x = counts_v[p, b, h * sub : (h + 1) * sub].reshape(sub_rows, k_local)
        inverse = pl.reciprocal(model, approx=True)
        ratio_high = (x * inverse).astype(BF16)
        ratio_low = ((x - model * ratio_high.astype(F32)) * inverse).astype(BF16)
        return ratio_high, ratio_low

    def collect(ratio_high, ratio_low):
        split = []
        for i in range(sub):
            split += [ratio_high[i * j_local : (i + 1) * j_local]]
            split += [ratio_low[i * j_local : (i + 1) * j_local]]
        inner = jnp.dot(
            jnp.concatenate(split, axis=0), c_out[...], preferred_element_type=F32
        ).reshape(sub, 2, j_local, 128)
        return jnp.sum((inner[:, 0] + inner[:, 1]) * norm_b[...][None], axis=1)

    def chunk(p, b):
        models = [expand(p, b, 0)]
        sums_of = []
        for h in range(pieces):
            if h + 1 < pieces:
                models.append(expand(p, b, h + 1))
            sums_of.append(collect(*divide(p, b, h, models[h])))
        part[b, p] = jnp.concatenate(sums_of, axis=0)

    def finish(u):
        b = lax.rem(u, blocks)
        wait_all(recv, rs_recv, b)

        @pl.when(u >= blocks)
        def _():
            wait_all(cur, ag_send, b)

        total = part[b, me]
        for d in range(1, group):
            total = total + recv[b, peer(d)]
        width = 64
        while width >= rank:
            total = total + pltpu.roll(total, width, 1)
            width //= 2
        cur[b, me] = cur[b, me] * (total / cells)

        @pl.when(u < (ITERS - 1) * blocks)
        def _():
            for d in range(1, group):
                send_cur(peer(d), me, b).start()

    steps = ITERS * blocks

    def step(s, carry):
        b = lax.rem(s, blocks)

        @pl.when(s < blocks)
        def _():
            load(b).wait()

        @pl.when(s >= blocks)
        def _():
            wait_all(cur, ag_recv, b)
            wait_all(part, rs_send, b)

        def one(d, carry):
            p = peer(d)
            chunk(p, b)

            @pl.when(d < group)
            def _():
                send_part(p, me, b).start()

            return carry

        lax.fori_loop(1, group // 2 + 1, one, 0)
        if blocks > 1:

            @pl.when(s >= 1)
            def _():
                finish(s - 1)

        lax.fori_loop(group // 2 + 1, group + 1, one, 0)
        if blocks == 1:
            finish(s)
        return carry

    lax.fori_loop(0, steps, step, 0)
    if blocks > 1:
        finish(steps - 1)
    for b in range(blocks):
        wait_all(part, rs_send, b)
        out_ref[b * rows : (b + 1) * rows, :] = cur[b, me][:, 0:rank]


def per_device(counts, factor_a, factor_b, factor_c):
    cols, tms = lax.axis_size("col"), lax.axis_size("tm")
    group = cols * tms
    rows_local, j_local, k_local = counts.shape
    rank = factor_a.shape[1]
    own = rows_local // group
    blocks = 2 if own % 16 == 0 else 1
    rows = own // blocks
    pieces = max(1, rows // 2)
    counts = counts.reshape(group, blocks, rows, j_local, k_local)
    cells = rows_local * j_local * k_local
    vmem = pl.BlockSpec(memory_space=pltpu.VMEM)
    dma = pltpu.SemaphoreType.DMA
    return pl.pallas_call(
        functools.partial(kernel, cols, tms, blocks, rows, pieces),
        out_shape=jax.ShapeDtypeStruct((own, rank), F32),
        in_specs=[pl.BlockSpec(memory_space=pltpu.HBM)] * 4,
        out_specs=vmem,
        scratch_shapes=[
            pltpu.VMEM((rank, rows_local), F32),
            pltpu.VMEM(factor_b.shape, F32),
            pltpu.VMEM((rank, k_local), F32),
            pltpu.VMEM(counts.shape, F32),
            pltpu.VMEM((blocks, group, rows, 128), F32),
            pltpu.VMEM((blocks, group, rows, 128), F32),
            pltpu.VMEM((blocks, group, rows, 128), F32),
            pltpu.VMEM((group, 8, 128), F32),
            pltpu.VMEM((tms, j_local // tms, 128), F32),
            pltpu.VMEM((j_local, 128), F32),
            pltpu.VMEM((128, k_local), BF16),
            pltpu.VMEM((k_local, 128), BF16),
            dma((3,)),
            dma((blocks,)),
            dma((group,)),
            dma((group,)),
            dma((tms,)),
            dma((tms,)),
            dma((blocks,)),
            dma((blocks,)),
            dma((blocks,)),
            dma((blocks,)),
        ],
        compiler_params=pltpu.CompilerParams(
            collective_id=0, has_side_effects=True, vmem_limit_bytes=48 * 1024 * 1024
        ),
        cost_estimate=pl.CostEstimate(
            flops=4 * ITERS * cells * rank,
            bytes_accessed=4 * cells,
            transcendentals=ITERS * cells,
        ),
    )(counts, factor_a.T, factor_b, factor_c.T)


def solution(mesh):
    return jax.shard_map(
        per_device,
        mesh=mesh,
        in_specs=(P("row", "col", "tm"), P("row", None), P(("col", "tm"), None), P("tm", None)),
        out_specs=P(("row", "col", "tm"), None),
        check_vma=False,
    )
```
